256 devices in a mesh: dp: 64 (over y, z, core), mp: 4 (over x).
Axes of the slice: x: 4, y: 4, z: 8, core: 2. Of those that a mesh axis runs over, the one named last changes fastest.
Arguments:
- acts: bfloat16 [32768, 8192], P('dp'), may hold values from -6 to 6
- grad_out: bfloat16 [32768, 8192], P('dp', 'mp'), may hold values from -0.03125 to 0.03125
- projector: bfloat16 [8192, 1024], P('dp', 'mp'), may hold values from -0.0625 to 0.0625
- moment1: float32 [1024, 8192], P('dp', 'mp'), may hold values from -2 to 2
- moment2: float32 [1024, 8192], P('dp', 'mp'), may hold values from 0.0005 to 0.05
Outputs:
- update: bfloat16 [8192, 8192], P('dp', 'mp')
- new_moment1: float32 [1024, 8192], P('dp', 'mp')
- new_moment2: float32 [1024, 8192], P('dp', 'mp')
The draws below stay inside these ranges and needn't reach their ends.
All inputs are finite; a program needn't handle non-finite values.
Results may differ from the reference program's by a relative error of at most 0.009.
Values may be sent and summed in bfloat16 or wider, within the bound.
No kernel may reach another device: no remote copies, remote signals or barrier semaphores. Data moves between devices by JAX's collectives and lax.ppermute only.
A program may use at most 128 MiB of HBM per device.

```python
import math
import jax
import jax.numpy as jnp
from jax import lax

D = 8192
RANK = 1024
TOKENS = 32768


def shard_levels(own_key, extent, shards, least, high):
    factor_of = 1.0
    for position, blocks in shards:
        steps = jax.random.uniform(jax.random.fold_in(jax.random.fold_in(own_key, 6), position), (blocks,), jnp.float32, least / len(shards), high / len(shards))
        factor_of = factor_of * jnp.repeat(jnp.exp(steps), extent[position] // blocks).reshape((-1,) + (1,) * (len(extent) - 1 - position))
    return factor_of


def scatter_about(rng, extent, width, limit, split=(), held_as=jnp.bfloat16):
    entries = width * jax.random.normal(rng, extent, jnp.float32)
    if split:
        entries = entries * shard_levels(rng, extent, split, -0.22, 0.18)
    return jnp.clip(entries, -limit, limit).astype(held_as)


def setup_inputs(seed: int = 0) -> dict:
    arg_keys = jax.random.split(jax.random.key(seed), 6)
    return {
        "acts": scatter_about(arg_keys[0], (TOKENS, D), 1.0, 6.0, ((0, 64),)),
        "grad_out": scatter_about(arg_keys[1], (TOKENS, D), TOKENS ** -0.5, 0.03125, ((0, 64), (1, 4))),
        "projector": scatter_about(arg_keys[2], (D, RANK), D ** -0.5, 0.0625, ((0, 64), (1, 4))),
        "moment1": scatter_about(arg_keys[3], (RANK, D), 0.3, 2.0, ((0, 64), (1, 4)), jnp.float32),
        "moment2": jnp.clip(jnp.exp(math.log(0.05) - 4.6051702 * jax.random.uniform(arg_keys[4], (RANK, D), jnp.float32) ** shard_levels(arg_keys[4], (RANK, D), ((0, 64), (1, 4)), -0.2, 0.2)), 0.0005, 0.05),
    }


first_fix = 1.0 - 0.9 ** 10
second_fix = 1.0 - 0.999 ** 10

def reference(acts, grad_out, projector, moment1, moment2):
    projected = jnp.dot(acts, projector, preferred_element_type=jnp.float32).astype(jnp.bfloat16)
    low_grad = lax.dot_general(projected, grad_out, (((0,), (0,)), ((), ())), preferred_element_type=jnp.float32)
    new_moment1 = 0.9 * moment1 + 0.1 * low_grad
    new_moment2 = 0.999 * moment2 + 0.001 * low_grad * low_grad
    direction = (new_moment1 / first_fix / (jnp.sqrt(new_moment2 / second_fix) + 1e-08)).astype(jnp.bfloat16)
    update = jnp.dot(projector, direction, preferred_element_type=jnp.float32).astype(jnp.bfloat16)
    return (update, new_moment1, new_moment2)
```

```python
import functools

import jax
import jax.numpy as jnp
from jax import lax
from jax.experimental import pallas as pl
from jax.experimental.pallas import tpu as pltpu
from jax.sharding import PartitionSpec as P

first_fix = 1.0 - 0.9**10
second_fix = 1.0 - 0.999**10

NY, NZ, NX = 4, 8, 4
BF, F32 = jnp.bfloat16, jnp.float32
VMEM_LIMIT = 40 * 1024 * 1024


def dp_permute(x, to):
    pairs = []
    for y in range(NY):
        for z in range(NZ):
            for c in range(2):
                ty, tz, tc = to(y, z, c)
                pairs.append(((y * NZ + z) * 2 + c, ((ty % NY) * NZ + tz % NZ) * 2 + tc))
    return lax.ppermute(x, "dp", pairs)


def from_y(x, o):
    return dp_permute(x, lambda y, z, c: (y - o, z, c))


def along_lane(x):
    return dp_permute(x, lambda y, z, c: (y, z + 1 - 2 * c, c))


def swap(x):
    return dp_permute(x, lambda y, z, c: (y, z, 1 - c))


def from_x(x, o):
    return lax.ppermute(x, "mp", [(i, (i - o) % NX) for i in range(NX)])


def at(x, i):
    return lax.dynamic_index_in_dim(x, i, 0, keepdims=False)


def gather(shard, c):
    own = jnp.stack([shard] + [from_y(shard, o) for o in range(1, NY)])
    other = swap(own)
    both = jnp.concatenate(
        [jnp.where(c == 0, own, other), jnp.where(c == 0, other, own)], axis=1
    )
    streams = [both[:2], both[2:]]
    mine, theirs = [[] for _ in range(3)], [[] for _ in range(3)]
    last = []
    for stream in streams:
        moving = stream
        for k in range(3):
            moving = along_lane(moving)
            mine[k].append(moving)
            theirs[k].append(swap(moving))
        half = along_lane(lax.dynamic_slice_in_dim(moving, c, 1, 0))
        other_half = swap(half)
        last.append(
            jnp.concatenate(
                [jnp.where(c == 0, half, other_half), jnp.where(c == 0, other_half, half)], axis=0
            )
        )
    return [streams] + mine + theirs + [last]


def project_kernel(n, first, idx, *refs):
    acts, pieces = refs[:NY], refs[NY : NY + 2 * n]
    refs = refs[NY + 2 * n :]
    start = None if first else refs[0]
    out, total = refs[-2:]
    k = pl.program_id(0)

    for i in range(n):

        @pl.when(k == i)
        def _():
            acc = sum(
                jnp.dot(
                    acts[o][...], pieces[2 * i + o // 2][o % 2], preferred_element_type=F32
                )
                for o in range(NY)
            )
            if i > 0:
                total[...] += acc
            elif first:
                total[...] = acc
            else:
                total[...] = start[...] + acc
            if i == n - 1:
                out[...] = total[...].astype(out.dtype)


def project(acts, pieces, zs, ys, start, dtype):
    n = len(pieces)
    tokens = acts.shape[0]
    wide = pieces[0][0].shape[1]
    columns = pieces[0][0].shape[2]
    idx = jnp.stack(list(zs) + list(ys)).astype(jnp.int32)
    flat = [p for pair in pieces for p in pair]
    whole = lambda p: pl.BlockSpec(p.shape, lambda k, idx, r=p.ndim: (0,) * r)
    extra = [] if start is None else [start]
    return pl.pallas_call(
        functools.partial(project_kernel, n, start is None),
        grid_spec=pltpu.PrefetchScalarGridSpec(
            num_scalar_prefetch=1,
            grid=(n,),
            in_specs=[
                pl.BlockSpec((tokens, wide), lambda k, idx, o=o: (0, idx[n + o] * NZ + idx[k]))
                for o in range(NY)
            ]
            + [whole(p) for p in flat + extra],
            out_specs=pl.BlockSpec((tokens, columns), lambda k, idx: (0, 0)),
            scratch_shapes=[pltpu.VMEM((tokens, columns), F32)],
        ),
        out_shape=jax.ShapeDtypeStruct((tokens, columns), dtype),
        compiler_params=pltpu.CompilerParams(vmem_limit_bytes=VMEM_LIMIT),
        cost_estimate=pl.CostEstimate(
            flops=2 * n * NY * tokens * wide * columns,
            bytes_accessed=2 * n * NY * wide * (tokens + columns),
            transcendentals=0,
        ),
    )(idx, *([acts] * NY), *flat, *extra)


def low_grad_kernel(a, b, grad, out):
    o = pl.program_id(1)
    for i, ref in enumerate((a, b)):

        @pl.when(o == i)
        def _():
            part = lax.dot_general(
                ref[...], grad[...], (((0,), (0,)), ((), ())), preferred_element_type=F32
            )
            out[...] = part.astype(BF).reshape(out.shape)


def low_grad_part(a, b, grad):
    tokens, ranks = a.shape
    columns = grad.shape[1]
    rows = ranks // NZ
    tile = columns // 2
    return pl.pallas_call(
        low_grad_kernel,
        grid=(2, 2),
        in_specs=[
            pl.BlockSpec((tokens, ranks), lambda j, o: (0, 0)),
            pl.BlockSpec((tokens, ranks), lambda j, o: (0, 0)),
            pl.BlockSpec((tokens, tile), lambda j, o: (0, j)),
        ],
        out_specs=pl.BlockSpec((NZ, 1, rows, tile), lambda j, o: (0, o, 0, j)),
        out_shape=jax.ShapeDtypeStruct((NZ, 2, rows, columns), BF),
        compiler_params=pltpu.CompilerParams(vmem_limit_bytes=VMEM_LIMIT),
        cost_estimate=pl.CostEstimate(
            flops=4 * tokens * ranks * columns,
            bytes_accessed=2 * (2 * tokens * ranks + tokens * columns + 2 * ranks * columns),
            transcendentals=0,
        ),
    )(a, b, grad)


def reduce_z(part, z, c):
    s = 1 - 2 * c
    block = lambda k: at(part, lax.rem(z + s * k + 2 * NZ, NZ))
    half = lambda b, i: lax.dynamic_slice_in_dim(b, i, 1, 0)
    far = block(4)
    far_other = swap(jnp.concatenate([half(far, 1 - c), block(-3)], axis=0))
    near_other = swap(jnp.concatenate([block(-2), block(-1)], axis=0))
    moving = along_lane((half(far, c).astype(F32) + far_other[:1].astype(F32)).astype(BF))
    zero = jnp.zeros_like(moving)
    moving = jnp.concatenate(
        [jnp.where(c == 0, moving, zero), jnp.where(c == 0, zero, moving)], axis=0
    )
    for k, other in ((3, far_other[1:]), (2, near_other[:2]), (1, near_other[2:])):
        moving = along_lane(
            (block(k).astype(F32) + other.astype(F32) + moving.astype(F32)).astype(BF)
        )
    total = block(0).astype(F32) + moving.astype(F32)
    rows = total.shape[1] // 2
    lower, upper = total[:, :rows], total[:, rows:]
    kept = jnp.where(c == 0, lower, upper)
    given = jnp.where(c == 0, upper, lower).astype(BF)
    return kept + swap(given).astype(F32)


def update_kernel(n, first, idx, *refs):
    rows_t, pieces = refs[0], refs[1 : 1 + 2 * n]
    refs = refs[1 + 2 * n :]
    out = refs[-1]
    acc = None if first else refs[0][...]
    for i in range(n):
        left = jnp.concatenate([rows_t[idx[n + o], idx[i]] for o in range(NY)], axis=0)
        right = jnp.concatenate([pieces[2 * i + o // 2][o % 2] for o in range(NY)], axis=0)
        part = lax.dot_general(left, right, (((0,), (0,)), ((), ())), preferred_element_type=F32)
        acc = part if acc is None else acc + part
    out[...] = acc.astype(out.dtype)


def update_part(rows_t, pieces, zs, xs, start, dtype):
    n = len(pieces)
    rows = rows_t.shape[-1]
    ranks, columns = pieces[0][0].shape[1:]
    tile = columns // 4
    idx = jnp.stack(list(zs) + list(xs)).astype(jnp.int32)
    flat = [p for pair in pieces for p in pair]
    extra = [] if start is None else [start]
    return pl.pallas_call(
        functools.partial(update_kernel, n, start is None),
        grid_spec=pltpu.PrefetchScalarGridSpec(
            num_scalar_prefetch=1,
            grid=(4,),
            in_specs=[pl.BlockSpec(rows_t.shape, lambda j, idx: (0, 0, 0, 0))]
            + [pl.BlockSpec((2, ranks, tile), lambda j, idx: (0, 0, j)) for _ in flat]
            + [pl.BlockSpec((rows, tile), lambda j, idx: (0, j)) for _ in extra],
            out_specs=pl.BlockSpec((rows, tile), lambda j, idx: (0, j)),
        ),
        out_shape=jax.ShapeDtypeStruct((rows, columns), dtype),
        compiler_params=pltpu.CompilerParams(vmem_limit_bytes=VMEM_LIMIT),
        cost_estimate=pl.CostEstimate(
            flops=2 * n * NY * ranks * rows * columns,
            bytes_accessed=2 * n * NY * ranks * columns + 4 * rows * columns,
            transcendentals=0,
        ),
    )(idx, rows_t, *flat, *extra)


def body(acts, grad_out, projector, moment1, moment2):
    dp = lax.axis_index("dp")
    x = lax.axis_index("mp")
    c = lax.rem(dp, 2)
    z = lax.rem(dp // 2, NZ)
    y = dp // (2 * NZ)
    s = 1 - 2 * c
    zs = [lax.rem(z + s * k + 2 * NZ, NZ) for k in (0, -1, -2, -3, 1, 2, 3, 4)]
    ys = [lax.rem(y + o, NY) for o in range(NY)]

    with jax.named_scope("gather_projector"):
        pieces = gather(projector, c)
    with jax.named_scope("project"):
        early = project(acts, pieces[:7], zs[:7], ys, None, F32)
        projected = project(acts, pieces[7:], zs[7:], ys, early, BF)

    with jax.named_scope("low_grad"):
        near = from_x(projected, 1)
        first = low_grad_part(projected, near, grad_out)
        second = low_grad_part(from_x(projected, 2), from_x(projected, 3), grad_out)
    with jax.named_scope("reduce"):
        summed = jnp.concatenate([reduce_z(first, z, c), reduce_z(second, z, c)], axis=0)
        owner = lambda d: at(summed, lax.rem(y + d - x + 2 * NY, NY))
        low_grad = owner(0)
        for d in range(1, NY):
            low_grad = low_grad + from_y(owner(d).astype(BF), -d).astype(F32)

    with jax.named_scope("adam"):
        new_moment1 = 0.9 * moment1 + 0.1 * low_grad
        new_moment2 = 0.999 * moment2 + 0.001 * low_grad * low_grad
        direction = (
            new_moment1 / first_fix / (jnp.sqrt(new_moment2 / second_fix) + 1e-08)
        ).astype(BF)

    with jax.named_scope("rows"):
        mine_t = projector.T
        rows_t = jnp.stack([mine_t] + [from_x(mine_t, o) for o in range(1, NX)])
        rows_t = rows_t.reshape(NX, NZ, -1, mine_t.shape[1])
        xs = [lax.rem(y + o - x + 2 * NX, NX) for o in range(NY)]

    with jax.named_scope("gather_direction"):
        pieces = gather(direction, c)
    with jax.named_scope("update"):
        early = update_part(rows_t, pieces[:7], zs[:7], xs, None, F32)
        update = update_part(rows_t, pieces[7:], zs[7:], xs, early, BF)
    return (update, new_moment1, new_moment2)


def solution(mesh):
    in_specs = (P("dp", None), P("dp", "mp"), P("dp", "mp"), P("dp", "mp"), P("dp", "mp"))
    out_specs = (P("dp", "mp"), P("dp", "mp"), P("dp", "mp"))
    return jax.shard_map(body, mesh=mesh, in_specs=in_specs, out_specs=out_specs, check_vma=False)
```

```python
import functools

import jax
import jax.numpy as jnp
from jax import lax
from jax.experimental import pallas as pl
from jax.experimental.pallas import tpu as pltpu
from jax.sharding import PartitionSpec as P

first_fix = 1.0 - 0.9**10
second_fix = 1.0 - 0.999**10

NY, NZ, NX = 4, 8, 4
BF, F32 = jnp.bfloat16, jnp.float32
VMEM_LIMIT = 16 * 1024 * 1024


def dp_permute(x, to):
    pairs = []
    for y in range(NY):
        for z in range(NZ):
            for c in range(2):
                ty, tz, tc = to(y, z, c)
                pairs.append(((y * NZ + z) * 2 + c, ((ty % NY) * NZ + tz % NZ) * 2 + tc))
    return lax.ppermute(x, "dp", pairs)


def from_y(x, o):
    return dp_permute(x, lambda y, z, c: (y - o, z, c))


def along_lane(x):
    return dp_permute(x, lambda y, z, c: (y, z + 1 - 2 * c, c))


def swap(x):
    return dp_permute(x, lambda y, z, c: (y, z, 1 - c))


def z_of(here, k):
    return lax.rem(here[2] + (1 - 2 * here[3]) * k + 2 * NZ, NZ)


def y_of(here, o):
    return lax.rem(here[1] + o, NY)


def core_of(here, core):
    return 0 if core is None else lax.rem(here[3] + core, 2)


def from_x(x, o):
    return lax.ppermute(x, "mp", [(i, (i - o) % NX) for i in range(NX)])


def at(x, i):
    return lax.dynamic_index_in_dim(x, i, 0, keepdims=False)


def whole():
    return pl.BlockSpec(memory_space=pltpu.VMEM)


def params():
    return pltpu.CompilerParams(vmem_limit_bytes=VMEM_LIMIT)


def tie(*xs):
    return lax.optimization_barrier(xs)


def pair_kernel(here, own0, own1, other0, other1, out):
    rows, c = own0.shape[0], here[3]
    mine = pl.ds(pl.multiple_of(c * rows, 16), rows)
    theirs = pl.ds(pl.multiple_of((1 - c) * rows, 16), rows)
    out[0, mine], out[1, mine] = own0[...], own1[...]
    out[0, theirs], out[1, theirs] = other0[...], other1[...]


def pair_up(here, owns, others):
    rows, columns = owns[0].shape
    return pl.pallas_call(
        pair_kernel,
        in_specs=[pl.BlockSpec(memory_space=pltpu.SMEM)] + [whole()] * 4,
        out_specs=whole(),
        out_shape=jax.ShapeDtypeStruct((2, 2 * rows, columns), BF),
        compiler_params=params(),
    )(here, *owns, *others)


def half_kernel(here, block, out):
    rows, c = out.shape[1], here[3]
    out[...] = block[:, pl.ds(pl.multiple_of(c * rows, 16), rows)]


def half_rows(here, block):
    count, rows, columns = block.shape
    return pl.pallas_call(
        half_kernel,
        in_specs=[pl.BlockSpec(memory_space=pltpu.SMEM), whole()],
        out_specs=whole(),
        out_shape=jax.ShapeDtypeStruct((count, rows // 2, columns), BF),
        compiler_params=params(),
    )(here, block)


def gather(shard, here, absorb, early):
    shards = [shard] + [from_y(shard, o) for o in range(1, NY)]
    others = [swap(own) for own in shards]
    moving = [pair_up(here, shards[i : i + 2], others[i : i + 2]) for i in (0, 2)]
    places = lambda blocks, k, core=None: [(b, 2 * i, k, core) for i, b in enumerate(blocks)]
    ready = places(moving, 0)
    theirs = [None, None]
    acc = None
    for k in range(1, 5):
        for i in range(2):
            got = along_lane(half_rows(here, moving[i]) if k == 4 else moving[i])
            if k > 1:
                got, theirs[i] = tie(got, theirs[i])
            if i == 1 and (k == 4 or k == 3 and early):
                got, acc = tie(got, acc)
            moving[i] = got
        if k > 1:
            ready += places(theirs, k - 1)
        if k < 4:
            ready += places(moving, -k)
        if k == 3 or k == 2 and early:
            acc = absorb(acc, ready, False)
            ready = []
        theirs = [swap(m) for m in moving]
    if early:
        acc = absorb(acc, ready, False)
        theirs[1], acc = tie(theirs[1], acc)
        ready = []
    return absorb(acc, ready + places(moving, 4, 0) + places(theirs, 4, 1), True)


def project_kernel(n, places_of, here, acts, *refs):
    pieces, out, scratch, sems = refs[:n], *refs[-3:]
    start = refs[n] if len(refs) > n + 3 else None
    tail = refs[n + 1] if len(refs) > n + 4 else None
    copies, places = [], [0]
    for i, piece in enumerate(pieces):
        width = piece.shape[1]
        o, k, core = places_of[i]
        for j in range(2):
            block = (y_of(here, o + j) * NZ + z_of(here, k)) * 2 + core_of(here, core)
            copies.append(
                pltpu.make_async_copy(
                    acts.at[:, pl.ds(pl.multiple_of(block * 128, 128), width)],
                    scratch.at[:, pl.ds(places[-1] + j * width, width)],
                    sems.at[2 * i + j],
                )
            )
            copies[-1].start()
        places.append(places[-1] + 2 * width)
    total = None if start is None else start[...]
    for g in range(0, n, 2):
        end = min(n, g + 2)
        for copy in copies[2 * g : 2 * end]:
            copy.wait()
        right = jnp.concatenate([p[j] for p in pieces[g:end] for j in range(2)], axis=0)
        left = scratch[:, pl.ds(places[g], places[end] - places[g])]
        part = jnp.dot(left, right, preferred_element_type=F32)
        total = part if total is None else total + part
    out[: total.shape[0]] = total.astype(out.dtype)
    if tail is not None:
        out[total.shape[0] :] = tail[...]


def project(here, acts, start, ready, tail):
    n = len(ready)
    pieces = [r[0] for r in ready]
    tokens, ranks = acts.shape[0], pieces[0].shape[2]
    depth = sum(2 * p.shape[1] for p in pieces)
    extra = [x for x in (start, tail) if x is not None]
    rows, dtype = (tokens, F32) if tail is None else (tokens + tail.shape[0], BF)
    return pl.pallas_call(
        functools.partial(project_kernel, n, [r[1:] for r in ready]),
        in_specs=[
            pl.BlockSpec(memory_space=pltpu.SMEM),
            pl.BlockSpec(memory_space=pltpu.HBM),
        ]
        + [whole()] * (n + len(extra)),
        out_specs=whole(),
        out_shape=jax.ShapeDtypeStruct((rows, ranks), dtype),
        scratch_shapes=[
            pltpu.VMEM((tokens, depth), BF),
            pltpu.SemaphoreType.DMA((2 * n,)),
        ],
        compiler_params=params(),
        cost_estimate=pl.CostEstimate(
            flops=2 * depth * tokens * ranks,
            bytes_accessed=2 * depth * (tokens + ranks),
            transcendentals=0,
        ),
    )(here, acts, *pieces, *extra)


def low_grad_kernel(a, grad, out):
    columns = grad.shape[1]
    tile = columns // 4
    for j in range(4):
        cut = pl.ds(j * tile, tile)
        part = lax.dot_general(
            a[: grad.shape[0]], grad[:, cut], (((0,), (0,)), ((), ())), preferred_element_type=F32
        )
        out[:, :, cut] = part.astype(BF).reshape(out.shape[0], out.shape[1], tile)


def low_grad_part(a, grad):
    ranks = a.shape[1]
    tokens, columns = grad.shape
    return pl.pallas_call(
        low_grad_kernel,
        in_specs=[whole(), whole()],
        out_specs=whole(),
        out_shape=jax.ShapeDtypeStruct((NZ, ranks // NZ, columns), BF),
        compiler_params=params(),
        cost_estimate=pl.CostEstimate(
            flops=2 * tokens * ranks * columns,
            bytes_accessed=2 * (tokens * ranks + tokens * columns + ranks * columns),
            transcendentals=0,
        ),
    )(a, grad)


def reduce_z(parts, z, c):
    s = 1 - 2 * c
    rows = parts[0].shape[1] // 2
    block = lambda k: jnp.stack([at(p, lax.rem(z + s * k + 2 * NZ, NZ)) for p in parts])
    half = lambda b, i: lax.dynamic_slice_in_dim(b, i * rows, rows, 1)
    far = block(4)
    far_other = swap(jnp.concatenate([half(far, 1 - c), block(-3)], axis=1))
    near_other = swap(jnp.concatenate([block(-2), block(-1)], axis=1))
    moving = along_lane((half(far, c).astype(F32) + far_other[:, :rows].astype(F32)).astype(BF))
    zero = jnp.zeros_like(moving)
    moving = jnp.concatenate(
        [jnp.where(c == 0, moving, zero), jnp.where(c == 0, zero, moving)], axis=1
    )
    others = (far_other[:, rows:], near_other[:, : 2 * rows], near_other[:, 2 * rows :])
    for k, other in zip((3, 2, 1), others):
        moving = along_lane(
            (block(k).astype(F32) + other.astype(F32) + moving.astype(F32)).astype(BF)
        )
    total = block(0).astype(F32) + moving.astype(F32)
    lower, upper = total[:, :rows], total[:, rows:]
    kept = jnp.where(c == 0, lower, upper)
    given = jnp.where(c == 0, upper, lower).astype(BF)
    return kept + swap(given).astype(F32)


def update_kernel(n, places_of, here, *refs):
    blocks, pieces = refs[:NX], refs[NX : NX + n]
    start = refs[NX + n] if len(refs) == NX + n + 3 else None
    out, stacked = refs[-2:]
    for o in range(NX):
        rows = blocks[o][blocks[o].shape[0] - out.shape[0] :]
        stacked[o] = rows.T.reshape(stacked.shape[1:])
    left = []
    for piece, (o, k, core) in zip(pieces, places_of):
        depth = piece.shape[1]
        for j in range(2):
            x = lax.rem(here[1] + o + j - here[0] + 2 * NX, NX)
            cut = pl.ds(pl.multiple_of(core_of(here, core) * depth, 16), depth)
            left.append(stacked[x, z_of(here, k), cut])
    left = jnp.concatenate(left, axis=0)
    tile = out.shape[1] // 4
    for t in range(4):
        cut = pl.ds(t * tile, tile)
        right = jnp.concatenate([p[j, :, cut] for p in pieces for j in range(2)], axis=0)
        part = lax.dot_general(left, right, (((0,), (0,)), ((), ())), preferred_element_type=F32)
        if start is not None:
            part = start[:, cut] + part
        out[:, cut] = part.astype(out.dtype)


def update_part(here, blocks, start, ready, rows, dtype):
    n = len(ready)
    pieces = [r[0] for r in ready]
    ranks = blocks[0].shape[1]
    columns = pieces[0].shape[2]
    depth = sum(2 * p.shape[1] for p in pieces)
    extra = [] if start is None else [start]
    return pl.pallas_call(
        functools.partial(update_kernel, n, [r[1:] for r in ready]),
        in_specs=[pl.BlockSpec(memory_space=pltpu.SMEM)] + [whole()] * (NX + n + len(extra)),
        out_specs=whole(),
        out_shape=jax.ShapeDtypeStruct((rows, columns), dtype),
        scratch_shapes=[pltpu.VMEM((NX, NZ, ranks // NZ, rows), BF)],
        compiler_params=params(),
        cost_estimate=pl.CostEstimate(
            flops=2 * depth * rows * columns,
            bytes_accessed=2 * depth * columns + 4 * rows * columns,
            transcendentals=0,
        ),
    )(here, *blocks, *pieces, *extra)


def body(acts, grad_out, projector, moment1, moment2):
    dp = lax.axis_index("dp")
    x = lax.axis_index("mp")
    c = lax.rem(dp, 2)
    z = lax.rem(dp // 2, NZ)
    y = dp // (2 * NZ)
    here = jnp.stack([x, y, z, c]).astype(jnp.int32)
    held = pltpu.with_memory_space_constraint(acts, pltpu.HBM)

    def absorb_projector(acc, ready, last):
        return project(here, held, acc, ready, projector if last else None)

    with jax.named_scope("projected"):
        projected = gather(projector, here, absorb_projector, True)

    with jax.named_scope("low_grad"):
        blocks = [projected] + [from_x(projected, o) for o in range(1, NX)]
        parts = [low_grad_part(b, grad_out) for b in blocks]
    with jax.named_scope("reduce"):
        summed = jnp.concatenate([reduce_z(parts[:2], z, c), reduce_z(parts[2:], z, c)], axis=0)
        owner = lambda d: at(summed, lax.rem(y + d - x + 2 * NY, NY))
        low_grad = owner(0)
        for d in range(1, NY):
            low_grad = low_grad + from_y(owner(d).astype(BF), -d).astype(F32)

    with jax.named_scope("adam"):
        new_moment1 = 0.9 * moment1 + 0.1 * low_grad
        new_moment2 = 0.999 * moment2 + 0.001 * low_grad * low_grad
        direction = (
            new_moment1 / first_fix / (jnp.sqrt(new_moment2 / second_fix) + 1e-08)
        ).astype(BF)

    def absorb_direction(acc, ready, last):
        return update_part(here, blocks, acc, ready, projector.shape[0], BF if last else F32)

    with jax.named_scope("update"):
        update = gather(direction, here, absorb_direction, False)
    return (update, new_moment1, new_moment2)


def solution(mesh):
    in_specs = (P("dp", None), P("dp", "mp"), P("dp", "mp"), P("dp", "mp"), P("dp", "mp"))
    out_specs = (P("dp", "mp"), P("dp", "mp"), P("dp", "mp"))
    return jax.shard_map(body, mesh=mesh, in_specs=in_specs, out_specs=out_specs, check_vma=False)
```

```python
import functools

import jax
import jax.numpy as jnp
from jax import lax
from jax.experimental import pallas as pl
from jax.experimental.pallas import tpu as pltpu
from jax.sharding import PartitionSpec as P

first_fix = 1.0 - 0.9**10
second_fix = 1.0 - 0.999**10

NY, NZ, NX = 4, 8, 4
BF, F32 = jnp.bfloat16, jnp.float32
VMEM_LIMIT = 16 * 1024 * 1024


def dp_permute(x, to):
    pairs = []
    for y in range(NY):
        for z in range(NZ):
            for c in range(2):
                ty, tz, tc = to(y, z, c)
                pairs.append(((y * NZ + z) * 2 + c, ((ty % NY) * NZ + tz % NZ) * 2 + tc))
    return lax.ppermute(x, "dp", pairs)


def from_y(x, o):
    return dp_permute(x, lambda y, z, c: (y - o, z, c))


def along_lane(x):
    return dp_permute(x, lambda y, z, c: (y, z + 1 - 2 * c, c))


def swap(x):
    return dp_permute(x, lambda y, z, c: (y, z, 1 - c))


def coordinates():
    dp = lax.axis_index("dp")
    return (
        lax.axis_index("mp"),
        lax.div(dp, 2 * NZ),
        lax.rem(lax.div(dp, 2), NZ),
        lax.rem(dp, 2),
    )


def z_of(here, k):
    return lax.rem(here[2] + (1 - 2 * here[3]) * k + 2 * NZ, NZ)


def y_of(here, o):
    return lax.rem(here[1] + o, NY)


def from_x(x, o):
    return lax.ppermute(x, "mp", [(i, (i - o) % NX) for i in range(NX)])


def at(x, i):
    return lax.dynamic_index_in_dim(x, i, 0, keepdims=False)


def whole():
    return pl.BlockSpec(memory_space=pltpu.VMEM)


def params():
    return pltpu.CompilerParams(vmem_limit_bytes=VMEM_LIMIT)


def pair_kernel(own0, own1, other0, other1, out):
    rows, c = own0.shape[0], coordinates()[3]
    mine = pl.ds(pl.multiple_of(c * rows, 16), rows)
    theirs = pl.ds(pl.multiple_of((1 - c) * rows, 16), rows)
    out[0, mine], out[1, mine] = own0[...], own1[...]
    out[0, theirs], out[1, theirs] = other0[...], other1[...]


def pair_up(owns, others):
    rows, columns = owns[0].shape
    return pl.pallas_call(
        pair_kernel,
        in_specs=[whole()] * 4,
        out_specs=whole(),
        out_shape=jax.ShapeDtypeStruct((2, 2 * rows, columns), BF),
        compiler_params=params(),
    )(*owns, *others)


def after_kernel(x, other, out):
    pass


def after(x, other):
    anywhere = pl.BlockSpec(memory_space=pl.ANY)
    return pl.pallas_call(
        after_kernel,
        in_specs=[anywhere, anywhere],
        out_specs=anywhere,
        out_shape=jax.ShapeDtypeStruct(x.shape, x.dtype),
        input_output_aliases={0: 0},
        compiler_params=params(),
    )(x, other)


def gather(shard, local, absorb, beside=None):
    shards = [shard] + [from_y(shard, o) for o in range(1, NY)]
    if beside is not None:
        shards[1] = after(shards[1], local)
    others = [swap(own) for own in shards]
    shards[0] = local
    moving = [pair_up(shards[i : i + 2], others[i : i + 2]) for i in (0, 2)]
    places = lambda blocks, k: [(b, 2 * i, k) for i, b in enumerate(blocks)]
    ready = places(moving, 0)
    acc, early = beside, beside is not None
    for k in range(1, 5):
        moving = [along_lane(m) for m in moving]
        if k == 1 and early:
            moving[0] = after(moving[0], beside)
        if k < 4:
            theirs = [swap(m) for m in moving]
            ready += places(moving, -k)
            if k > 1 or not early:
                later = places(theirs, k)
            if k == 1:
                ready += places(theirs, k)
                later = []
        if k == 3 or k == 2 and early:
            acc = absorb(acc, ready, False)
            ready = later
            if k == 3 and early:
                acc = absorb(acc, ready, False)
                ready = []
        elif k == 2:
            ready += later
    return absorb(acc, ready + places(moving, 4), True)


def load_kernel(a, out, sem):
    copy = pltpu.make_async_copy(a, out, sem)
    copy.start()
    copy.wait()


def load(a):
    return pl.pallas_call(
        load_kernel,
        in_specs=[pl.BlockSpec(memory_space=pltpu.HBM)],
        out_specs=whole(),
        out_shape=jax.ShapeDtypeStruct(a.shape, a.dtype),
        scratch_shapes=[pltpu.SemaphoreType.DMA],
        compiler_params=params(),
        cost_estimate=pl.CostEstimate(flops=0, bytes_accessed=4 * a.size, transcendentals=0),
    )(pltpu.with_memory_space_constraint(a, pltpu.HBM))


def project_kernel(n, places_of, acts, *refs):
    here = coordinates()
    pieces, out = refs[:n], refs[-1]
    start = refs[n] if len(refs) > n + 1 else None
    tail = refs[n + 1] if len(refs) > n + 2 else None
    left, right = [], []
    for piece, (o, k) in zip(pieces, places_of):
        width = piece.shape[1]
        for j in range(2):
            block = y_of(here, o + j) * NZ + z_of(here, k)
            left.append(acts[:, pl.ds(pl.multiple_of(block * width, width), width)])
            right.append(piece[j])
    total = jnp.dot(
        jnp.concatenate(left, axis=1),
        jnp.concatenate(right, axis=0),
        preferred_element_type=F32,
    )
    if start is not None:
        total = start[...] + total
    out[: total.shape[0]] = total.astype(out.dtype)
    if tail is not None:
        out[total.shape[0] :] = tail[...]


def project(acts, start, ready, tail):
    n = len(ready)
    pieces = [r[0] for r in ready]
    tokens, ranks = acts.shape[0], pieces[0].shape[2]
    depth = sum(2 * p.shape[1] for p in pieces)
    extra = [x for x in (start, tail) if x is not None]
    rows, dtype = (tokens, F32) if tail is None else (tokens + tail.shape[0], BF)
    return pl.pallas_call(
        functools.partial(project_kernel, n, [r[1:] for r in ready]),
        in_specs=[whole()] * (1 + n + len(extra)),
        out_specs=whole(),
        out_shape=jax.ShapeDtypeStruct((rows, ranks), dtype),
        compiler_params=params(),
        cost_estimate=pl.CostEstimate(
            flops=2 * depth * tokens * ranks,
            bytes_accessed=2 * depth * (tokens + ranks),
            transcendentals=0,
        ),
    )(acts, *pieces, *extra)


def low_grad_kernel(a, grad, out):
    columns = grad.shape[1]
    tile = columns // 4
    for j in range(4):
        cut = pl.ds(j * tile, tile)
        part = lax.dot_general(
            a[: grad.shape[0]], grad[:, cut], (((0,), (0,)), ((), ())), preferred_element_type=F32
        )
        out[:, :, cut] = part.astype(BF).reshape(out.shape[0], out.shape[1], tile)


def low_grad_part(a, grad):
    ranks = a.shape[1]
    tokens, columns = grad.shape
    return pl.pallas_call(
        low_grad_kernel,
        in_specs=[whole(), whole()],
        out_specs=whole(),
        out_shape=jax.ShapeDtypeStruct((NZ, ranks // NZ, columns), BF),
        compiler_params=params(),
        cost_estimate=pl.CostEstimate(
            flops=2 * tokens * ranks * columns,
            bytes_accessed=2 * (tokens * ranks + tokens * columns + ranks * columns),
            transcendentals=0,
        ),
    )(a, grad)


def reduce_z(parts, z, c):
    s = 1 - 2 * c
    rows = parts[0].shape[1] // 2
    block = lambda k: jnp.stack([at(p, lax.rem(z + s * k + 2 * NZ, NZ)) for p in parts])
    half = lambda b, i: lax.dynamic_slice_in_dim(b, i * rows, rows, 1)
    far = block(4)
    far_other = swap(jnp.concatenate([half(far, 1 - c), block(-3)], axis=1))
    near_other = swap(jnp.concatenate([block(-2), block(-1)], axis=1))
    moving = along_lane((half(far, c).astype(F32) + far_other[:, :rows].astype(F32)).astype(BF))
    zero = jnp.zeros_like(moving)
    moving = jnp.concatenate(
        [jnp.where(c == 0, moving, zero), jnp.where(c == 0, zero, moving)], axis=1
    )
    others = (far_other[:, rows:], near_other[:, : 2 * rows], near_other[:, 2 * rows :])
    for k, other in zip((3, 2, 1), others):
        moving = along_lane(
            (block(k).astype(F32) + other.astype(F32) + moving.astype(F32)).astype(BF)
        )
    total = block(0).astype(F32) + moving.astype(F32)
    lower, upper = total[:, :rows], total[:, rows:]
    kept = jnp.where(c == 0, lower, upper)
    given = jnp.where(c == 0, upper, lower).astype(BF)
    return kept + swap(given).astype(F32)


def update_kernel(n, places_of, *refs):
    here = coordinates()
    blocks, pieces = refs[:NX], refs[NX : NX + n]
    start = refs[NX + n] if len(refs) == NX + n + 3 else None
    out, stacked = refs[-2:]
    for o in range(NX):
        rows = blocks[o][blocks[o].shape[0] - out.shape[0] :]
        stacked[o] = rows.T.reshape(stacked.shape[1:])
    left = []
    for o, k in places_of:
        for j in range(2):
            x = lax.rem(here[1] + o + j - here[0] + 2 * NX, NX)
            left.append(stacked[x, z_of(here, k)])
    left = jnp.concatenate(left, axis=0)
    tile = out.shape[1] // 4
    for t in range(4):
        cut = pl.ds(t * tile, tile)
        right = jnp.concatenate([p[j, :, cut] for p in pieces for j in range(2)], axis=0)
        part = lax.dot_general(left, right, (((0,), (0,)), ((), ())), preferred_element_type=F32)
        if start is not None:
            part = start[:, cut] + part
        out[:, cut] = part.astype(out.dtype)


def update_part(blocks, start, ready, rows, dtype):
    n = len(ready)
    pieces = [r[0] for r in ready]
    ranks = blocks[0].shape[1]
    columns = pieces[0].shape[2]
    depth = sum(2 * p.shape[1] for p in pieces)
    extra = [] if start is None else [start]
    return pl.pallas_call(
        functools.partial(update_kernel, n, [r[1:] for r in ready]),
        in_specs=[whole()] * (NX + n + len(extra)),
        out_specs=whole(),
        out_shape=jax.ShapeDtypeStruct((rows, columns), dtype),
        scratch_shapes=[pltpu.VMEM((NX, NZ, ranks // NZ, rows), BF)],
        compiler_params=params(),
        cost_estimate=pl.CostEstimate(
            flops=2 * depth * rows * columns,
            bytes_accessed=2 * depth * columns + 4 * rows * columns,
            transcendentals=0,
        ),
    )(*blocks, *pieces, *extra)


def body(acts, grad_out, projector, moment1, moment2):
    x, y, z, c = coordinates()
    local = load(projector)

    def absorb_projector(acc, ready, last):
        held, acc = acc if isinstance(acc, tuple) else (acc, None)
        acc = project(held, acc, ready, local if last else None)
        return acc if last else (held, acc)

    with jax.named_scope("projected"):
        projected = gather(projector, local, absorb_projector, load(acts))

    with jax.named_scope("low_grad"):
        blocks = [projected] + [from_x(projected, o) for o in range(1, NX)]
        parts = [low_grad_part(b, grad_out) for b in blocks]
    with jax.named_scope("reduce"):
        summed = jnp.concatenate([reduce_z(parts[:2], z, c), reduce_z(parts[2:], z, c)], axis=0)
        owner = lambda d: at(summed, lax.rem(y + d - x + 2 * NY, NY))
        low_grad = owner(0)
        for d in range(1, NY):
            low_grad = low_grad + from_y(owner(d).astype(BF), -d).astype(F32)

    with jax.named_scope("adam"):
        new_moment1 = 0.9 * moment1 + 0.1 * low_grad
        new_moment2 = 0.999 * moment2 + 0.001 * low_grad * low_grad
        direction = (
            new_moment1 / first_fix / (jnp.sqrt(new_moment2 / second_fix) + 1e-08)
        ).astype(BF)

    def absorb_direction(acc, ready, last):
        return update_part(blocks, acc, ready, projector.shape[0], BF if last else F32)

    with jax.named_scope("update"):
        update = gather(direction, direction, absorb_direction)
    return (update, new_moment1, new_moment2)


def solution(mesh):
    in_specs = (P("dp", None), P("dp", "mp"), P("dp", "mp"), P("dp", "mp"), P("dp", "mp"))
    out_specs = (P("dp", "mp"), P("dp", "mp"), P("dp", "mp"))
    return jax.shard_map(body, mesh=mesh, in_specs=in_specs, out_specs=out_specs, check_vma=False)
```

```python
import functools

import jax
import jax.numpy as jnp
from jax import lax
from jax.experimental import pallas as pl
from jax.experimental.pallas import tpu as pltpu
from jax.sharding import PartitionSpec as P

first_fix = 1.0 - 0.9**10
second_fix = 1.0 - 0.999**10

NY, NZ, NX = 4, 8, 4
BF, F32 = jnp.bfloat16, jnp.float32
VMEM_LIMIT = 16 * 1024 * 1024


def dp_permute(x, to):
    pairs = []
    for y in range(NY):
        for z in range(NZ):
            for c in range(2):
                ty, tz, tc = to(y, z, c)
                pairs.append(((y * NZ + z) * 2 + c, ((ty % NY) * NZ + tz % NZ) * 2 + tc))
    return lax.ppermute(x, "dp", pairs)


def from_y(x, o):
    return dp_permute(x, lambda y, z, c: (y - o, z, c))


def along_lane(x):
    return dp_permute(x, lambda y, z, c: (y, z + 1 - 2 * c, c))


def across(x):
    return dp_permute(x, lambda y, z, c: (y, z + NZ // 2, c))


def swap(x):
    return dp_permute(x, lambda y, z, c: (y, z, 1 - c))


def coordinates():
    dp = lax.axis_index("dp")
    return (
        lax.axis_index("mp"),
        lax.div(dp, 2 * NZ),
        lax.rem(lax.div(dp, 2), NZ),
        lax.rem(dp, 2),
    )


def z_of(here, k):
    return lax.rem(here[2] + (1 - 2 * here[3]) * k + 2 * NZ, NZ)


def y_of(here, o):
    return lax.rem(here[1] + o, NY)


def from_x(x, o):
    return lax.ppermute(x, "mp", [(i, (i - o) % NX) for i in range(NX)])


def at(x, i):
    return lax.dynamic_index_in_dim(x, i, 0, keepdims=False)


def whole():
    return pl.BlockSpec(memory_space=pltpu.VMEM)


def params():
    return pltpu.CompilerParams(vmem_limit_bytes=VMEM_LIMIT)


def pair_kernel(own0, own1, other0, other1, out):
    rows, c = own0.shape[0], coordinates()[3]
    mine = pl.ds(pl.multiple_of(c * rows, 16), rows)
    theirs = pl.ds(pl.multiple_of((1 - c) * rows, 16), rows)
    out[0, mine], out[1, mine] = own0[...], own1[...]
    out[0, theirs], out[1, theirs] = other0[...], other1[...]


def pair_up(owns, others):
    rows, columns = owns[0].shape
    return pl.pallas_call(
        pair_kernel,
        in_specs=[whole()] * 4,
        out_specs=whole(),
        out_shape=jax.ShapeDtypeStruct((2, 2 * rows, columns), BF),
        compiler_params=params(),
    )(*owns, *others)


def after_kernel(x, other, out):
    pass


def after(x, other):
    anywhere = pl.BlockSpec(memory_space=pl.ANY)
    return pl.pallas_call(
        after_kernel,
        in_specs=[anywhere, anywhere],
        out_specs=anywhere,
        out_shape=jax.ShapeDtypeStruct(x.shape, x.dtype),
        input_output_aliases={0: 0},
        compiler_params=params(),
    )(x, other)


def gather(shard, local, absorb, beside=None):
    shards = [shard] + [from_y(shard, o) for o in range(1, NY)]
    if beside is not None:
        shards[1] = after(shards[1], local)
    others = [swap(own) for own in shards]
    shards[0] = local
    moving = [pair_up(shards[i : i + 2], others[i : i + 2]) for i in (0, 2)]
    places = lambda blocks, k: [(b, 2 * i, k) for i, b in enumerate(blocks)]
    ready = places(moving, 0)
    acc, early = beside, beside is not None
    for k in range(1, 5):
        moving = [along_lane(m) for m in moving]
        if k == 1 and early:
            moving[0] = after(moving[0], beside)
        if k < 4:
            theirs = [swap(m) for m in moving]
            ready += places(moving, -k)
            if k > 1 or not early:
                later = places(theirs, k)
            if k == 1:
                ready += places(theirs, k)
                later = []
        if k == 3 or k == 2 and early:
            acc = absorb(acc, ready, False)
            ready = later
            if k == 3 and early:
                acc = absorb(acc, ready, False)
                ready = []
        elif k == 2:
            ready += later
    return absorb(acc, ready + places(moving, 4), True)


def gather_beside(shard, absorb):
    shards = [shard] + [from_y(shard, o) for o in range(1, NY)]
    pairs = lambda owns, others: [pair_up(owns[i : i + 2], others[i : i + 2]) for i in (0, 2)]
    moving = pairs(shards, [swap(own) for own in shards])
    fars = [across(shard)]
    places = lambda blocks, k: [(b, 2 * i, k) for i, b in enumerate(blocks)]
    ready = places(moving, 0)
    for k in range(1, 4):
        moving = [along_lane(m) for m in moving]
        if k == 1:
            moving[0] = after(moving[0], fars[0])
            fars += [from_y(fars[0], o) for o in range(1, NY)]
        if k == 2:
            for far in fars[1:]:
                moving[0] = after(moving[0], far)
        ready += places(moving, -k) + places([swap(m) for m in moving], k)
        if k == 2:
            far_pairs = pairs(fars, [swap(far) for far in fars])
            acc = absorb(None, ready, False)
            ready = places(far_pairs, 4)
    return absorb(acc, ready, True)


def load_kernel(a, out, sem):
    copy = pltpu.make_async_copy(a, out, sem)
    copy.start()
    copy.wait()


def load(a):
    return pl.pallas_call(
        load_kernel,
        in_specs=[pl.BlockSpec(memory_space=pltpu.HBM)],
        out_specs=whole(),
        out_shape=jax.ShapeDtypeStruct(a.shape, a.dtype),
        scratch_shapes=[pltpu.SemaphoreType.DMA],
        compiler_params=params(),
        cost_estimate=pl.CostEstimate(flops=0, bytes_accessed=4 * a.size, transcendentals=0),
    )(pltpu.with_memory_space_constraint(a, pltpu.HBM))


def project_kernel(n, places_of, acts, *refs):
    here = coordinates()
    pieces, out = refs[:n], refs[-1]
    start = refs[n] if len(refs) > n + 1 else None
    tail = refs[n + 1] if len(refs) > n + 2 else None
    left, right = [], []
    for piece, (o, k) in zip(pieces, places_of):
        width = piece.shape[1]
        for j in range(2):
            block = y_of(here, o + j) * NZ + z_of(here, k)
            left.append(acts[:, pl.ds(pl.multiple_of(block * width, width), width)])
            right.append(piece[j])
    total = jnp.dot(
        jnp.concatenate(left, axis=1),
        jnp.concatenate(right, axis=0),
        preferred_element_type=F32,
    )
    if start is not None:
        total = start[...] + total
    out[: total.shape[0]] = total.astype(out.dtype)
    if tail is not None:
        out[total.shape[0] :] = tail[...]


def project(acts, start, ready, tail):
    n = len(ready)
    pieces = [r[0] for r in ready]
    tokens, ranks = acts.shape[0], pieces[0].shape[2]
    depth = sum(2 * p.shape[1] for p in pieces)
    extra = [x for x in (start, tail) if x is not None]
    rows, dtype = (tokens, F32) if tail is None else (tokens + tail.shape[0], BF)
    return pl.pallas_call(
        functools.partial(project_kernel, n, [r[1:] for r in ready]),
        in_specs=[whole()] * (1 + n + len(extra)),
        out_specs=whole(),
        out_shape=jax.ShapeDtypeStruct((rows, ranks), dtype),
        compiler_params=params(),
        cost_estimate=pl.CostEstimate(
            flops=2 * depth * tokens * ranks,
            bytes_accessed=2 * depth * (tokens + ranks),
            transcendentals=0,
        ),
    )(acts, *pieces, *extra)


def low_grad_kernel(a, grad, out):
    columns = grad.shape[1]
    tile = columns // 4
    for j in range(4):
        cut = pl.ds(j * tile, tile)
        part = lax.dot_general(
            a[: grad.shape[0]], grad[:, cut], (((0,), (0,)), ((), ())), preferred_element_type=F32
        )
        out[:, :, cut] = part.astype(BF).reshape(out.shape[0], out.shape[1], tile)


def low_grad_part(a, grad):
    ranks = a.shape[1]
    tokens, columns = grad.shape
    return pl.pallas_call(
        low_grad_kernel,
        in_specs=[whole(), whole()],
        out_specs=whole(),
        out_shape=jax.ShapeDtypeStruct((NZ, ranks // NZ, columns), BF),
        compiler_params=params(),
        cost_estimate=pl.CostEstimate(
            flops=2 * tokens * ranks * columns,
            bytes_accessed=2 * (tokens * ranks + tokens * columns + ranks * columns),
            transcendentals=0,
        ),
    )(a, grad)


def reduce_z(parts, z, c):
    s = 1 - 2 * c
    rows = parts[0].shape[1] // 2
    block = lambda k: jnp.stack([at(p, lax.rem(z + s * k + 2 * NZ, NZ)) for p in parts])
    moving = along_lane(block(4))
    far_other = swap(block(-3))
    near_other = swap(jnp.concatenate([block(-2), block(-1)], axis=1))
    others = (far_other, near_other[:, : 2 * rows], near_other[:, 2 * rows :])
    for k, other in zip((3, 2, 1), others):
        moving = along_lane(
            (block(k).astype(F32) + other.astype(F32) + moving.astype(F32)).astype(BF)
        )
    total = block(0).astype(F32) + moving.astype(F32)
    lower, upper = total[:, :rows], total[:, rows:]
    kept = jnp.where(c == 0, lower, upper)
    given = jnp.where(c == 0, upper, lower).astype(BF)
    return kept + swap(given).astype(F32)


def update_kernel(n, places_of, *refs):
    here = coordinates()
    blocks, pieces = refs[:NX], refs[NX : NX + n]
    start = refs[NX + n] if len(refs) == NX + n + 3 else None
    out, stacked = refs[-2:]
    for o in range(NX):
        rows = blocks[o][blocks[o].shape[0] - out.shape[0] :]
        stacked[o] = rows.T.reshape(stacked.shape[1:])
    left = []
    for o, k in places_of:
        for j in range(2):
            x = lax.rem(here[1] + o + j - here[0] + 2 * NX, NX)
            left.append(stacked[x, z_of(here, k)])
    left = jnp.concatenate(left, axis=0)
    tile = out.shape[1] // 4
    for t in range(4):
        cut = pl.ds(t * tile, tile)
        right = jnp.concatenate([p[j, :, cut] for p in pieces for j in range(2)], axis=0)
        part = lax.dot_general(left, right, (((0,), (0,)), ((), ())), preferred_element_type=F32)
        if start is not None:
            part = start[:, cut] + part
        out[:, cut] = part.astype(out.dtype)


def update_part(blocks, start, ready, rows, dtype):
    n = len(ready)
    pieces = [r[0] for r in ready]
    ranks = blocks[0].shape[1]
    columns = pieces[0].shape[2]
    depth = sum(2 * p.shape[1] for p in pieces)
    extra = [] if start is None else [start]
    return pl.pallas_call(
        functools.partial(update_kernel, n, [r[1:] for r in ready]),
        in_specs=[whole()] * (NX + n + len(extra)),
        out_specs=whole(),
        out_shape=jax.ShapeDtypeStruct((rows, columns), dtype),
        scratch_shapes=[pltpu.VMEM((NX, NZ, ranks // NZ, rows), BF)],
        compiler_params=params(),
        cost_estimate=pl.CostEstimate(
            flops=2 * depth * rows * columns,
            bytes_accessed=2 * depth * columns + 4 * rows * columns,
            transcendentals=0,
        ),
    )(*blocks, *pieces, *extra)


def body(acts, grad_out, projector, moment1, moment2):
    x, y, z, c = coordinates()
    local = load(projector)

    def absorb_projector(acc, ready, last):
        held, acc = acc if isinstance(acc, tuple) else (acc, None)
        acc = project(held, acc, ready, local if last else None)
        return acc if last else (held, acc)

    with jax.named_scope("projected"):
        projected = gather(projector, local, absorb_projector, load(acts))

    with jax.named_scope("low_grad"):
        blocks = [projected] + [from_x(projected, o) for o in range(1, NX)]
        parts = [low_grad_part(b, grad_out) for b in blocks]
    with jax.named_scope("reduce"):
        summed = jnp.concatenate([reduce_z(parts[:2], z, c), reduce_z(parts[2:], z, c)], axis=0)
        owner = lambda d: at(summed, lax.rem(y + d - x + 2 * NY, NY))
        low_grad = owner(0)
        for d in range(1, NY):
            low_grad = low_grad + from_y(owner(d).astype(BF), -d).astype(F32)

    with jax.named_scope("adam"):
        new_moment1 = 0.9 * moment1 + 0.1 * low_grad
        new_moment2 = 0.999 * moment2 + 0.001 * low_grad * low_grad
        direction = (
            new_moment1 / first_fix / (jnp.sqrt(new_moment2 / second_fix) + 1e-08)
        ).astype(BF)

    def absorb_direction(acc, ready, last):
        return update_part(blocks, acc, ready, projector.shape[0], BF if last else F32)

    with jax.named_scope("update"):
        update = gather_beside(direction, absorb_direction)
    return (update, new_moment1, new_moment2)


def solution(mesh):
    in_specs = (P("dp", None), P("dp", "mp"), P("dp", "mp"), P("dp", "mp"), P("dp", "mp"))
    out_specs = (P("dp", "mp"), P("dp", "mp"), P("dp", "mp"))
    return jax.shard_map(body, mesh=mesh, in_specs=in_specs, out_specs=out_specs, check_vma=False)
```

```python
import functools

import jax
import jax.numpy as jnp
from jax import lax
from jax.experimental import pallas as pl
from jax.experimental.pallas import tpu as pltpu
from jax.sharding import PartitionSpec as P

first_fix = 1.0 - 0.9**10
second_fix = 1.0 - 0.999**10

NY, NZ, NX = 4, 8, 4
BF, F32 = jnp.bfloat16, jnp.float32
VMEM_LIMIT = 16 * 1024 * 1024


def dp_permute(x, to):
    pairs = []
    for y in range(NY):
        for z in range(NZ):
            for c in range(2):
                ty, tz, tc = to(y, z, c)
                pairs.append(((y * NZ + z) * 2 + c, ((ty % NY) * NZ + tz % NZ) * 2 + tc))
    return lax.ppermute(x, "dp", pairs)


def from_y(x, o):
    return dp_permute(x, lambda y, z, c: (y - o, z, c))


def along_lane(x):
    return dp_permute(x, lambda y, z, c: (y, z + 1 - 2 * c, c))


def swap(x):
    return dp_permute(x, lambda y, z, c: (y, z, 1 - c))


def coordinates():
    dp = lax.axis_index("dp")
    return (
        lax.axis_index("mp"),
        lax.div(dp, 2 * NZ),
        lax.rem(lax.div(dp, 2), NZ),
        lax.rem(dp, 2),
    )


def z_of(here, k):
    return lax.rem(here[2] + (1 - 2 * here[3]) * k + 2 * NZ, NZ)


def y_of(here, o):
    return lax.rem(here[1] + o, NY)


def from_x(x, o):
    return lax.ppermute(x, "mp", [(i, (i - o) % NX) for i in range(NX)])


def at(x, i):
    return lax.dynamic_index_in_dim(x, i, 0, keepdims=False)


def whole():
    return pl.BlockSpec(memory_space=pltpu.VMEM)


def params():
    return pltpu.CompilerParams(vmem_limit_bytes=VMEM_LIMIT)


def pair_kernel(own0, own1, other0, other1, out):
    rows, c = own0.shape[0], coordinates()[3]
    mine = pl.ds(pl.multiple_of(c * rows, 16), rows)
    theirs = pl.ds(pl.multiple_of((1 - c) * rows, 16), rows)
    out[0, mine], out[1, mine] = own0[...], own1[...]
    out[0, theirs], out[1, theirs] = other0[...], other1[...]


def pair_up(owns, others):
    rows, columns = owns[0].shape
    return pl.pallas_call(
        pair_kernel,
        in_specs=[whole()] * 4,
        out_specs=whole(),
        out_shape=jax.ShapeDtypeStruct((2, 2 * rows, columns), BF),
        compiler_params=params(),
    )(*owns, *others)


def after_kernel(x, other, out):
    pass


def after(x, other):
    anywhere = pl.BlockSpec(memory_space=pl.ANY)
    return pl.pallas_call(
        after_kernel,
        in_specs=[anywhere, anywhere],
        out_specs=anywhere,
        out_shape=jax.ShapeDtypeStruct(x.shape, x.dtype),
        input_output_aliases={0: 0},
        compiler_params=params(),
    )(x, other)


def gather(shard, local, absorb, beside=None):
    shards = [shard] + [from_y(shard, o) for o in range(1, NY)]
    if beside is not None:
        shards[1] = after(shards[1], local)
    others = [swap(own) for own in shards]
    shards[0] = local
    moving = [pair_up(shards[i : i + 2], others[i : i + 2]) for i in (0, 2)]
    places = lambda blocks, k: [(b, 2 * i, k) for i, b in enumerate(blocks)]
    ready = places(moving, 0)
    acc, early = beside, beside is not None
    for k in range(1, 5):
        moving = [along_lane(m) for m in moving]
        if k == 1 and early:
            moving[0] = after(moving[0], beside)
        if k < 4:
            theirs = [swap(m) for m in moving]
            ready += places(moving, -k)
            if k > 1 or not early:
                later = places(theirs, k)
            if k == 1:
                ready += places(theirs, k)
                later = []
        if k == 3 or k == 2 and early:
            acc = absorb(acc, ready, False)
            ready = later
            if k == 3 and early:
                acc = absorb(acc, ready, False)
                ready = []
        elif k == 2:
            ready += later
    return absorb(acc, ready + places(moving, 4), True)


def load_kernel(a, out, sem):
    copy = pltpu.make_async_copy(a, out, sem)
    copy.start()
    copy.wait()


def load(a):
    return pl.pallas_call(
        load_kernel,
        in_specs=[pl.BlockSpec(memory_space=pltpu.HBM)],
        out_specs=whole(),
        out_shape=jax.ShapeDtypeStruct(a.shape, a.dtype),
        scratch_shapes=[pltpu.SemaphoreType.DMA],
        compiler_params=params(),
        cost_estimate=pl.CostEstimate(flops=0, bytes_accessed=4 * a.size, transcendentals=0),
    )(pltpu.with_memory_space_constraint(a, pltpu.HBM))


def project_kernel(n, places_of, acts, *refs):
    here = coordinates()
    pieces, out = refs[:n], refs[-1]
    start = refs[n] if len(refs) > n + 1 else None
    tail = refs[n + 1] if len(refs) > n + 2 else None
    left, right = [], []
    for piece, (o, k) in zip(pieces, places_of):
        width = piece.shape[1]
        for j in range(2):
            block = y_of(here, o + j) * NZ + z_of(here, k)
            left.append(acts[:, pl.ds(pl.multiple_of(block * width, width), width)])
            right.append(piece[j])
    total = jnp.dot(
        jnp.concatenate(left, axis=1),
        jnp.concatenate(right, axis=0),
        preferred_element_type=F32,
    )
    if start is not None:
        total = start[...] + total
    out[: total.shape[0]] = total.astype(out.dtype)
    if tail is not None:
        out[total.shape[0] :] = tail[...]


def project(acts, start, ready, tail):
    n = len(ready)
    pieces = [r[0] for r in ready]
    tokens, ranks = acts.shape[0], pieces[0].shape[2]
    depth = sum(2 * p.shape[1] for p in pieces)
    extra = [x for x in (start, tail) if x is not None]
    rows, dtype = (tokens, F32) if tail is None else (tokens + tail.shape[0], BF)
    return pl.pallas_call(
        functools.partial(project_kernel, n, [r[1:] for r in ready]),
        in_specs=[whole()] * (1 + n + len(extra)),
        out_specs=whole(),
        out_shape=jax.ShapeDtypeStruct((rows, ranks), dtype),
        compiler_params=params(),
        cost_estimate=pl.CostEstimate(
            flops=2 * depth * tokens * ranks,
            bytes_accessed=2 * depth * (tokens + ranks),
            transcendentals=0,
        ),
    )(acts, *pieces, *extra)


def low_grad_kernel(a, grad, out):
    columns = grad.shape[1]
    tile = columns // 4
    for j in range(4):
        cut = pl.ds(j * tile, tile)
        part = lax.dot_general(
            a[: grad.shape[0]], grad[:, cut], (((0,), (0,)), ((), ())), preferred_element_type=F32
        )
        out[:, :, cut] = part.astype(BF).reshape(out.shape[0], out.shape[1], tile)


def low_grad_part(a, grad):
    ranks = a.shape[1]
    tokens, columns = grad.shape
    return pl.pallas_call(
        low_grad_kernel,
        in_specs=[whole(), whole()],
        out_specs=whole(),
        out_shape=jax.ShapeDtypeStruct((NZ, ranks // NZ, columns), BF),
        compiler_params=params(),
        cost_estimate=pl.CostEstimate(
            flops=2 * tokens * ranks * columns,
            bytes_accessed=2 * (tokens * ranks + tokens * columns + ranks * columns),
            transcendentals=0,
        ),
    )(a, grad)


def reduce_z(parts, z, c):
    s = 1 - 2 * c
    rows = parts[0].shape[1] // 2
    block = lambda k: jnp.stack([at(p, lax.rem(z + s * k + 2 * NZ, NZ)) for p in parts])
    moving = along_lane(block(4))
    far_other = swap(block(-3))
    near_other = swap(jnp.concatenate([block(-2), block(-1)], axis=1))
    others = (far_other, near_other[:, : 2 * rows], near_other[:, 2 * rows :])
    for k, other in zip((3, 2, 1), others):
        moving = along_lane(
            (block(k).astype(F32) + other.astype(F32) + moving.astype(F32)).astype(BF)
        )
    total = block(0).astype(F32) + moving.astype(F32)
    lower, upper = total[:, :rows], total[:, rows:]
    kept = jnp.where(c == 0, lower, upper)
    given = jnp.where(c == 0, upper, lower).astype(BF)
    return kept + swap(given).astype(F32)


def update_kernel(n, places_of, *refs):
    here = coordinates()
    blocks, pieces = refs[:NX], refs[NX : NX + n]
    start = refs[NX + n] if len(refs) == NX + n + 3 else None
    out, stacked = refs[-2:]
    for o in range(NX):
        rows = blocks[o][blocks[o].shape[0] - out.shape[0] :]
        stacked[o] = rows.T.reshape(stacked.shape[1:])
    left = []
    for o, k in places_of:
        for j in range(2):
            x = lax.rem(here[1] + o + j - here[0] + 2 * NX, NX)
            left.append(stacked[x, z_of(here, k)])
    left = jnp.concatenate(left, axis=0)
    tile = out.shape[1] // 4
    for t in range(4):
        cut = pl.ds(t * tile, tile)
        right = jnp.concatenate([p[j, :, cut] for p in pieces for j in range(2)], axis=0)
        part = lax.dot_general(left, right, (((0,), (0,)), ((), ())), preferred_element_type=F32)
        if start is not None:
            part = start[:, cut] + part
        out[:, cut] = part.astype(out.dtype)


def update_part(blocks, start, ready, rows, dtype):
    n = len(ready)
    pieces = [r[0] for r in ready]
    ranks = blocks[0].shape[1]
    columns = pieces[0].shape[2]
    depth = sum(2 * p.shape[1] for p in pieces)
    extra = [] if start is None else [start]
    return pl.pallas_call(
        functools.partial(update_kernel, n, [r[1:] for r in ready]),
        in_specs=[whole()] * (NX + n + len(extra)),
        out_specs=whole(),
        out_shape=jax.ShapeDtypeStruct((rows, columns), dtype),
        scratch_shapes=[pltpu.VMEM((NX, NZ, ranks // NZ, rows), BF)],
        compiler_params=params(),
        cost_estimate=pl.CostEstimate(
            flops=2 * depth * rows * columns,
            bytes_accessed=2 * depth * columns + 4 * rows * columns,
            transcendentals=0,
        ),
    )(*blocks, *pieces, *extra)


def body(acts, grad_out, projector, moment1, moment2):
    x, y, z, c = coordinates()
    local = load(projector)

    def absorb_projector(acc, ready, last):
        held, acc = acc if isinstance(acc, tuple) else (acc, None)
        acc = project(held, acc, ready, local if last else None)
        return acc if last else (held, acc)

    with jax.named_scope("projected"):
        projected = gather(projector, local, absorb_projector, load(acts))

    with jax.named_scope("low_grad"):
        blocks = [projected] + [from_x(projected, o) for o in range(1, NX)]
        parts = [low_grad_part(b, grad_out) for b in blocks]
    with jax.named_scope("reduce"):
        summed = jnp.concatenate([reduce_z(parts[:2], z, c), reduce_z(parts[2:], z, c)], axis=0)
        owner = lambda d: at(summed, lax.rem(y + d - x + 2 * NY, NY))
        low_grad = owner(0)
        for d in range(1, NY):
            low_grad = low_grad + from_y(owner(d).astype(BF), -d).astype(F32)

    with jax.named_scope("adam"):
        new_moment1 = 0.9 * moment1 + 0.1 * low_grad
        new_moment2 = 0.999 * moment2 + 0.001 * low_grad * low_grad
        direction = (
            new_moment1 / first_fix / (jnp.sqrt(new_moment2 / second_fix) + 1e-08)
        ).astype(BF)

    def absorb_direction(acc, ready, last):
        return update_part(blocks, acc, ready, projector.shape[0], BF if last else F32)

    with jax.named_scope("update"):
        update = gather(direction, direction, absorb_direction)
    return (update, new_moment1, new_moment2)


def solution(mesh):
    in_specs = (P("dp", None), P("dp", "mp"), P("dp", "mp"), P("dp", "mp"), P("dp", "mp"))
    out_specs = (P("dp", "mp"), P("dp", "mp"), P("dp", "mp"))
    return jax.shard_map(body, mesh=mesh, in_specs=in_specs, out_specs=out_specs, check_vma=False)
```
